256 devices in a mesh: rep: 8 (over x_lo, y), shard: 32 (over z, x_hi, core).
Axes of the slice: x: 4 (x_hi: 2, x_lo: 2; x = x_hi * 2 + x_lo), y: 4, z: 8, core: 2. Of those that a mesh axis runs over, the one named last changes fastest.
Arguments:
- tokens: bfloat16 [32768, 1024], P(('rep', 'shard')), may hold values from -6 to 6
- out_cotangent: bfloat16 [32768, 1024], P(('rep', 'shard')), may hold values from -6 to 6
- seq_lengths: int32 [256, 4], P(('rep', 'shard')), may hold values from 1 to 64, 128 in all within a row
- routes: int32 [32768, 8], P(('rep', 'shard')), may hold values from 0 to 11, all different within a row; in each aligned block of 128 rows (0 to 127, 128 to 255, ...) at most 102 rows name the same one
- gain_attn: bfloat16 [1024], P('shard'), may hold values from 0.099609375 to 1.8984375
- w_query: bfloat16 [1024, 1024], P('shard'), may hold values from -0.25 to 0.25
- w_key: bfloat16 [1024, 512], P('shard'), may hold values from -0.25 to 0.25
- w_value: bfloat16 [1024, 512], P('shard'), may hold values from -0.1875 to 0.1875
- w_out: bfloat16 [1024, 1024], P('shard'), may hold values from -0.5 to 0.5
- gain_ffn: bfloat16 [1024], P('shard'), may hold values from 0.099609375 to 1.8984375
- w_router: bfloat16 [1024, 12], P('shard'), may hold values from -0.09375 to 0.09375
- w_gate: bfloat16 [1024, 12, 512], P('shard'), may hold values from -0.1875 to 0.1875
- w_up: bfloat16 [1024, 12, 512], P('shard'), may hold values from -0.1875 to 0.1875
- w_down: bfloat16 [512, 12, 1024], P('shard'), may hold values from -1 to 1
Outputs:
- output: bfloat16 [32768, 1024], P(('rep', 'shard'))
- tokens_grad: float32 [32768, 1024], P(('rep', 'shard'))
- grad_gain_attn: float32 [1024], P('shard')
- grad_w_query: float32 [1024, 1024], P('shard')
- grad_w_key: float32 [1024, 512], P('shard')
- grad_w_value: float32 [1024, 512], P('shard')
- grad_w_out: float32 [1024, 1024], P('shard')
- grad_gain_ffn: float32 [1024], P('shard')
- grad_w_router: float32 [1024, 12], P('shard')
- grad_w_gate: float32 [1024, 12, 512], P('shard')
- grad_w_up: float32 [1024, 12, 512], P('shard')
- grad_w_down: float32 [512, 12, 1024], P('shard')
The draws below stay inside these ranges and needn't reach their ends.
Inputs may be any that keep to these rules, and one draw needn't show every extreme that they name: `seq_lengths`: each device's row lists the lengths of its 4 sequences in order; they sum to 128, and on every device the longest has exactly 64 tokens. `routes`: A token's 8 experts are distinct; among the 128 tokens of one device no expert is chosen more than 102 times, and on some devices one is chosen exactly 102 times.
All inputs are finite; a program needn't handle non-finite values.
Results may differ from the reference program's by a relative error of at most 0.024.
Values may be sent and summed in bfloat16 or wider, within the bound.
No kernel may reach another device: no remote copies, remote signals or barrier semaphores. Data moves between devices by JAX's collectives and lax.ppermute only.
A program may use at most 192 MiB of HBM per device.

```python
import math
from functools import partial
import jax
import jax.numpy as jnp
import numpy as np
from jax import lax

D = 1024
HEADS = 16
KV_HEADS = 8
HEAD_DIM = 64
F = 512
TOP = 8
EXPERTS = 12
TOK_DEV = 128
SEQS_DEV = 4
CAP = 102
TOKENS = 32768
N_REP = 8
N_SHARD = 32


def block_levels(key, shape, split, low, high):
    factor_of = 1.0
    for axis_at, shards_of in split:
        heights = jax.random.uniform(jax.random.fold_in(jax.random.fold_in(key, 6), axis_at), (shards_of,), jnp.float32, low / len(split), high / len(split))
        factor_of = factor_of * jnp.repeat(jnp.exp(heights), shape[axis_at] // shards_of).reshape((-1,) + (1,) * (len(shape) - 1 - axis_at))
    return factor_of


def profile(amount, total, bound, lean):
    weights = [(1 << 20) // math.isqrt(grade ** lean) + 1 for grade in range(2, amount + 1)]
    spare, holding = total - bound - (amount - 1), [1] * (amount - 1)
    while spare > 0:
        movable = [i for i in range(amount - 1) if holding[i] < bound]
        pool, budget = sum([weights[i] for i in movable]), spare
        for i in movable:
            extra = min(bound - holding[i], max(1, budget * weights[i] // pool), spare)
            holding[i] = holding[i] + extra
            spare = spare - extra
    return np.array([bound] + holding)


def ragged(own_key, amount, total, reach, slope):
    if amount == 2:
        one = jax.random.randint(own_key, (), max(1, total - reach), min(reach, total - 1) + 1)
        return jnp.stack([one, total - one])
    sizes = jnp.asarray(profile(amount, total, reach, slope), jnp.int32)
    couples = (amount - 1) // 2
    source_of, receiver = sizes[1:1 + 2 * couples:2], sizes[2:2 + 2 * couples:2]
    margin = jnp.minimum(source_of - 1, reach - receiver)
    moved = jax.random.randint(jax.random.fold_in(own_key, 1), (couples,), 0, 1 << 20) % (margin + 1)
    sizes = sizes.at[1:1 + 2 * couples:2].set(source_of - moved).at[2:2 + 2 * couples:2].set(receiver + moved)
    return sizes[jax.random.permutation(jax.random.fold_in(own_key, 2), amount)]


def deal_out(own_key, own, number, rows, count, top, limit, lean):
    order = jax.random.permutation(own_key, count)
    heavy_load, common = load_shares(count, rows * top, limit, lean, True), load_shares(count, rows * top, limit, lean, False)
    places = jnp.arange(count)

    def named(sizes, turn):
        used = int((sizes > 0).sum())
        fixed = max(1, used // 4)
        shifted = fixed + (places - fixed + turn * (used - fixed)) % max(1, count - fixed)
        return jnp.zeros((count,), jnp.int32).at[order[jnp.where(places < fixed, places, shifted)]].set(jnp.asarray(sizes, jnp.int32))

    sizes = jnp.where(number % 4 == 0, named(heavy_load, number // 4), named(common, number - number // 4 - 1))
    mixed = jax.random.permutation(jax.random.fold_in(own, 3), count)
    source_of, receiver = mixed[0:count // 2 * 2:2], mixed[1:count // 2 * 2:2]
    margin = jnp.minimum(sizes[source_of] - 1, limit - sizes[receiver]) // 2
    margin = jnp.where((source_of == order[0]) | (receiver == order[0]) | (sizes[receiver] == 0), 0, jnp.maximum(margin, 0))
    shifted = jax.random.randint(jax.random.fold_in(own, 4), (count // 2,), 0, 1 << 20) % (margin + 1)
    sizes = sizes.at[source_of].add(-shifted).at[receiver].add(shifted)
    labels = jnp.searchsorted(jnp.cumsum(sizes), jnp.arange(rows * top), side="right").astype(jnp.int32)
    listing = labels.reshape(top, rows).T
    listing = listing[jax.random.permutation(jax.random.fold_in(own, 1), rows)]
    turn = jax.random.randint(jax.random.fold_in(own, 2), (rows, 1), 0, top)
    return jnp.take_along_axis(listing, (jnp.arange(top)[None, :] + turn) % top, axis=1)


def load_shares(number_of, total, most, slope, full):
    portions = [(1 << 20) // math.isqrt(standing ** slope) + 1 for standing in range(1, number_of + 1)]
    largest = most if full else min(most, max(-(-total // number_of), total * portions[0] // sum(portions)))
    least = 1 if total - largest >= number_of - 1 else 0
    given, surplus = [largest] + [least] * (number_of - 1), total - largest - least * (number_of - 1)
    while surplus > 0:
        movable = [i for i in range(1, number_of) if given[i] < largest] or [i for i in range(1, number_of) if given[i] < most]
        pool, budget = sum([portions[i] for i in movable]), surplus
        for i in movable:
            more = min(most - given[i], max(1, budget * portions[i] // pool), surplus)
            given[i] = given[i] + more
            surplus = surplus - more
    return np.array(given)


def scatter_about(key, dims, deviation, reach, pieces=(), kind=jnp.bfloat16):
    array = jax.random.normal(key, dims, jnp.float32) * deviation
    if len(pieces) > 0:
        array = block_levels(key, dims, pieces, -0.22, 0.18) * array
    return jnp.clip(array, min=-reach, max=reach).astype(kind)


def setup_inputs(seed: int = 0) -> dict:
    arg_keys = jax.random.split(jax.random.key(seed), 15)
    tokens = scatter_about(arg_keys[0], (TOKENS, D), 1.0, 6.0, ((0, 256),))
    out_cotangent = scatter_about(arg_keys[1], (TOKENS, D), 1.0, 6.0, ((0, 256),))
    seq_lengths = jax.vmap(lambda own: ragged(own, SEQS_DEV, TOK_DEV, TOK_DEV // 2, 2))(jax.random.split(arg_keys[2], (N_REP * N_SHARD))).reshape((N_REP * N_SHARD, SEQS_DEV)).astype(jnp.int32)
    routes_keys = jax.random.split(jax.random.fold_in(arg_keys[3], 1), TOKENS // TOK_DEV)
    routes_turns = jax.random.permutation(jax.random.fold_in(arg_keys[3], 3), TOKENS // TOK_DEV)
    routes = jax.vmap(lambda own, number: deal_out(jax.random.fold_in(arg_keys[3], 2), own, number, TOK_DEV, EXPERTS, TOP, CAP, 1))(routes_keys, routes_turns).reshape((TOKENS, TOP))
    gain_attn = jnp.clip(1.0 + 0.18 * jax.random.normal(arg_keys[4], (D,), jnp.float32), 0.099609375, 1.8984375).astype(jnp.bfloat16)
    w_query = scatter_about(arg_keys[5], (D, HEADS * HEAD_DIM), (D // 2) ** -0.5, 0.25, ((0, 32),))
    w_key = scatter_about(arg_keys[6], (D, KV_HEADS * HEAD_DIM), (D // 2) ** -0.5, 0.25, ((0, 32),))
    w_value = scatter_about(arg_keys[7], (D, KV_HEADS * HEAD_DIM), D ** -0.5, 0.1875, ((0, 32),))
    w_out = scatter_about(arg_keys[8], (HEADS * HEAD_DIM, D), (D // 8) ** -0.5, 0.5, ((0, 32),))
    gain_ffn = jnp.clip(1.0 + 0.18 * jax.random.normal(arg_keys[9], (D,), jnp.float32), 0.099609375, 1.8984375).astype(jnp.bfloat16)
    w_router = scatter_about(arg_keys[10], (D, EXPERTS), (4 * D) ** -0.5, 0.09375, ((0, 32),))
    w_gate = scatter_about(arg_keys[11], (D, EXPERTS, F), D ** -0.5, 0.1875, ((0, 32),))
    w_up = scatter_about(arg_keys[12], (D, EXPERTS, F), D ** -0.5, 0.1875, ((0, 32),))
    w_down = scatter_about(arg_keys[13], (F, EXPERTS, D), (F // 16) ** -0.5, 1.0, ((0, 32),))
    return {"tokens": tokens, "out_cotangent": out_cotangent, "seq_lengths": seq_lengths, "routes": routes, "gain_attn": gain_attn, "w_query": w_query, "w_key": w_key, "w_value": w_value, "w_out": w_out, "gain_ffn": gain_ffn, "w_router": w_router, "w_gate": w_gate, "w_up": w_up, "w_down": w_down}


@jax.custom_vjp
def low(v):
    return lax.optimization_barrier(v.astype(jnp.bfloat16)).astype(jnp.float32)

@jax.custom_vjp
def low_back(v):
    return v

def low_keep(v):
    return (low(v), None)

def low_pass(kept, grad):
    return (grad,)

def back_keep(v):
    return (v, None)

def back_low(kept, grad):
    return (low(grad),)
low.defvjp(low_keep, low_pass)
low_back.defvjp(back_keep, back_low)
HIGHEST = lax.Precision.HIGHEST
EPSILON = 1e-06

def seq_layout(lengths):
    row_ids = jnp.arange(TOK_DEV, dtype=jnp.int32)
    lengths = lengths.astype(jnp.int32)
    seq_ends = jnp.cumsum(lengths).astype(jnp.int32)
    seq_starts = (seq_ends - lengths).astype(jnp.int32)
    segment = lax.optimization_barrier(jnp.sum((row_ids[:, None] >= seq_ends[None, :]).astype(jnp.int32), axis=1)).astype(jnp.int32)
    picked = segment[:, None] == jnp.arange(SEQS_DEV, dtype=jnp.int32)[None, :]
    positions = row_ids - lax.optimization_barrier(jnp.sum(jnp.where(picked, seq_starts[None, :], 0), axis=1)).astype(jnp.int32)
    allowed = (row_ids[None, :] <= row_ids[:, None]) & (segment[:, None] == segment[None, :])
    return (positions, allowed)

def rope_tables(positions):
    half_dim = HEAD_DIM // 2
    inverse = 10000.0 ** (-2.0 * jnp.arange(half_dim, dtype=jnp.float32) / HEAD_DIM)
    angles = positions.astype(jnp.float32)[..., None] * inverse
    return (jnp.cos(angles), jnp.sin(angles))

def rotate(values_in, cosine, sine_table):
    half_dim = values_in.shape[-1] // 2
    first_half = values_in[..., :half_dim]
    second_half = values_in[..., half_dim:]
    cosine = cosine[..., None, :]
    sine_table = sine_table[..., None, :]
    return jnp.concatenate([first_half * cosine - second_half * sine_table, second_half * cosine + first_half * sine_table], axis=-1)

def group_forward(params, inputs):
    tok_in, lengths, chosen_ids = inputs
    gain_attn, w_query, w_key, w_value, w_out, gain_ffn, w_router, w_gate, w_up, w_down = params
    groups_n = tok_in.shape[0]
    positions, allowed = jax.vmap(seq_layout)(lengths)
    cosine, sine_table = rope_tables(positions)
    inv_in = lax.rsqrt(lax.optimization_barrier(jnp.mean(tok_in * tok_in, axis=-1, keepdims=True)) + EPSILON)
    normed_in = low(tok_in * inv_in * gain_attn)
    query_raw = low_back(jnp.einsum('gtd,dq->gtq', normed_in, w_query, precision=HIGHEST))
    key_raw = low_back(jnp.einsum('gtd,dq->gtq', normed_in, w_key, precision=HIGHEST))
    value_raw = low_back(jnp.einsum('gtd,dq->gtq', normed_in, w_value, precision=HIGHEST))
    query_rot = low(rotate(query_raw.reshape(groups_n, TOK_DEV, HEADS, HEAD_DIM), cosine, sine_table) * HEAD_DIM ** (-0.5))
    key_rot = low(rotate(key_raw.reshape(groups_n, TOK_DEV, KV_HEADS, HEAD_DIM), cosine, sine_table))
    value_heads = low(value_raw.reshape(groups_n, TOK_DEV, KV_HEADS, HEAD_DIM))
    query_grouped = query_rot.reshape(groups_n, TOK_DEV, KV_HEADS, HEADS // KV_HEADS, HEAD_DIM)
    scores = low_back(jnp.einsum('gqkrd,gskd->gkrqs', query_grouped, key_rot, precision=HIGHEST))
    masked = jnp.where(allowed[:, None, None, :, :], scores, -1000000000.0)
    weights_low = low(jax.nn.softmax(masked, axis=-1))
    attended = jnp.einsum('gkrqs,gskd->gqkrd', weights_low, value_heads, precision=HIGHEST)
    attended = low(low_back(attended.reshape(groups_n, TOK_DEV, HEADS * HEAD_DIM)))
    mixed_res = tok_in + low_back(jnp.einsum('gtq,qd->gtd', attended, w_out, precision=HIGHEST))
    inv_mid = lax.rsqrt(lax.optimization_barrier(jnp.mean(mixed_res * mixed_res, axis=-1, keepdims=True)) + EPSILON)
    normed_mid = low(mixed_res * inv_mid * gain_ffn)
    logits = jnp.einsum('gtd,de->gte', normed_mid, w_router, precision=HIGHEST)
    onehot = chosen_ids[..., None] == jnp.arange(EXPERTS, dtype=jnp.int32)
    chosen = lax.optimization_barrier(jnp.sum(jnp.where(onehot, logits[:, :, None, :], 0.0), axis=-1))
    gate_weights = jax.nn.softmax(chosen, axis=-1)
    combine = lax.optimization_barrier(jnp.sum(jnp.where(onehot, gate_weights[..., None], 0.0), axis=2))

    def expert_step(running, expert):
        gate_w, up_w, down_w, share_e = expert
        gate_pre = low_back(jnp.einsum('gtd,df->gtf', normed_mid, gate_w, precision=HIGHEST))
        up_pre = low_back(jnp.einsum('gtd,df->gtf', normed_mid, up_w, precision=HIGHEST))
        hidden = low(jax.nn.silu(gate_pre) * up_pre)
        result = low_back(jnp.einsum('gtf,fd->gtd', hidden, down_w, precision=HIGHEST))
        return (running + share_e[..., None] * result, None)
    expert_inputs = (jnp.moveaxis(w_gate, 1, 0), jnp.moveaxis(w_up, 1, 0), jnp.moveaxis(w_down, 1, 0), jnp.moveaxis(combine, 2, 0))
    branch, unused_out = lax.scan(jax.checkpoint(expert_step), jnp.zeros_like(mixed_res), expert_inputs)
    return mixed_res + branch

def reference(tokens, out_cotangent, seq_lengths, routes, gain_attn, w_query, w_key, w_value, w_out, gain_ffn, w_router, w_gate, w_up, w_down):
    params = (gain_attn.astype(jnp.float32), w_query.astype(jnp.float32), w_key.astype(jnp.float32), w_value.astype(jnp.float32), w_out.astype(jnp.float32), gain_ffn.astype(jnp.float32), w_router.astype(jnp.float32), w_gate.astype(jnp.float32), w_up.astype(jnp.float32), w_down.astype(jnp.float32))
    devices_n = N_REP * N_SHARD
    group_size = math.gcd(devices_n, max(1, 4096 // TOK_DEV))
    blocks_n = devices_n // group_size

    def forward(weights_all, tok_all):
        inputs = (tok_all.reshape(blocks_n, group_size, TOK_DEV, D), seq_lengths.reshape(blocks_n, group_size, SEQS_DEV), routes.reshape(blocks_n, group_size, TOK_DEV, TOP))
        outputs = lax.map(jax.checkpoint(partial(group_forward, weights_all)), inputs)
        return outputs.reshape(devices_n * TOK_DEV, D)
    result, pullback = jax.vjp(forward, params, tokens.astype(jnp.float32))
    weight_grads, token_grad = pullback(out_cotangent.astype(jnp.float32))
    return (result.astype(jnp.bfloat16), token_grad, weight_grads[0], weight_grads[1], weight_grads[2], weight_grads[3], weight_grads[4], weight_grads[5], weight_grads[6], weight_grads[7], weight_grads[8], weight_grads[9])
```

```python
import jax
import jax.numpy as jnp
import numpy as np
from jax import lax
from jax.sharding import Mesh
from jax.sharding import PartitionSpec as P

HEADS = 16
KV_HEADS = 8
HEAD_DIM = 64
SHARD = ("z", "xh", "c")
REP_SHARD = ("xl", "yh", "yl", "z", "xh", "c")
CHIPS = ("xl", "yl")
APART = ("yh",)
GROUP = ("c", *CHIPS)
SIZES = {"xl": 2, "yh": 2, "yl": 2, "z": 8, "xh": 2, "c": 2}
N_CHIPS = 4
N_APART = 8 // N_CHIPS
N_C, N_XH = 2, 2
N_GROUP = N_CHIPS * N_C
MAX_LEN = 64
EPSILON = 1e-06
HIGHEST = lax.Precision.HIGHEST
BF = jnp.bfloat16
F32 = jnp.float32


def dot(a, b, ca, cb, precision=None):
    return lax.dot_general(
        a, b, (((ca,), (cb,)), ((), ())), precision=precision, preferred_element_type=F32
    )


def swap(x, axes):
    return lax.all_to_all(x, axes, 0, 0, tiled=False)


def gather_group(x):
    x = swap(jnp.broadcast_to(x[None], (N_CHIPS, *x.shape)), CHIPS)
    x = swap(jnp.broadcast_to(x[None], (N_C, *x.shape)), "c")
    return x.reshape(N_GROUP, *x.shape[2:])


def after(x, *others):
    for other in others:
        x = x + (other[(0,) * other.ndim] * 0).astype(x.dtype)
    return x


def scatter_group(x, first=(), second=()):
    x = x.reshape(N_C, N_CHIPS, *x.shape[1:])
    x = after(jnp.sum(swap(x, "c").astype(F32), axis=0), *first).astype(BF)
    return after(jnp.sum(swap(x, CHIPS).astype(F32), axis=0), *second)


def fetch_rows(x):
    x = swap(jnp.broadcast_to(x[None], (N_XH, *x.shape)).reshape(-1, *x.shape[1:]), ("xh", "c"))
    x = x.reshape(-1, x.shape[-1])
    return lax.all_gather(x, "z", axis=0, tiled=True)


def to_owners(x):
    rows = x.shape[1] // N_C
    x = jnp.broadcast_to(x[None], (N_APART, *x.shape))
    x = x.reshape(N_APART * N_XH, *x.shape[2:])
    x = jnp.sum(swap(x, (*APART, "xh")).astype(F32), axis=0).astype(BF)
    x = x.reshape(N_C, 1, rows, *x.shape[1:])
    x = jnp.broadcast_to(x, (N_C, N_CHIPS, *x.shape[2:])).reshape(N_GROUP, *x.shape[2:])
    return swap(x, GROUP)


def to_owners_at_once(x):
    rows = x.shape[1] // N_C
    x = x.reshape(1, 1, N_XH, N_C, rows, *x.shape[2:])
    x = jnp.broadcast_to(x, (N_APART, N_CHIPS, *x.shape[2:])).transpose(0, 2, 3, 1, 4, 5)
    x = swap(x.reshape(-1, *x.shape[4:]), (*APART, "xh", *GROUP))
    x = x.reshape(N_APART * N_XH, N_GROUP, *x.shape[1:])
    return jnp.sum(x.astype(F32), axis=0)


def on_device(
    tokens,
    out_cotangent,
    seq_lengths,
    routes,
    gain_attn,
    w_query,
    w_key,
    w_value,
    w_out,
    gain_ffn,
    w_router,
    w_gate,
    w_up,
    w_down,
):
    rows, model_w = tokens.shape
    experts_n = w_router.shape[1]
    hidden_w = w_gate.shape[2]
    own_d = w_gate.shape[0]
    group_t = rows * N_GROUP
    kv_w = HEAD_DIM
    q_w = HEADS // KV_HEADS * HEAD_DIM
    qk_w = q_w + kv_w
    qkv_w = qk_w + kv_w
    out_w = model_w // N_GROUP
    part_f = hidden_w // N_GROUP
    spread = experts_n * part_f
    own_f = w_down.shape[0]
    part_down = own_f // N_GROUP
    y_at = lax.axis_index(CHIPS)

    def columns(w, width):
        return jnp.stack(
            [
                lax.dynamic_slice_in_dim(w, (k * N_CHIPS + y_at) * width, width, axis=1)
                for k in range(N_C)
            ]
        )

    aux_w = jnp.concatenate(
        [
            gain_attn[:, None],
            gain_ffn[:, None],
            w_router,
            jnp.zeros((own_d, 128 - 2 - experts_n), BF),
        ],
        axis=1,
    )
    dense_own = jnp.concatenate(
        [
            columns(w_query, q_w),
            columns(w_key, kv_w),
            columns(w_value, kv_w),
            columns(w_out, out_w),
            jnp.broadcast_to(aux_w[None], (N_C, own_d, 128)),
        ],
        axis=2,
    )
    dense = fetch_rows(dense_own)
    f_ids = jnp.arange(hidden_w, dtype=jnp.int32)[:, None]
    s_ids = jnp.arange(N_C * part_f, dtype=jnp.int32)[None, :]
    k_ids = s_ids % part_f
    picked_f = (
        own_f * (k_ids // part_down)
        + part_down * (s_ids // part_f * N_CHIPS + y_at)
        + k_ids % part_down
    )
    select = (f_ids == picked_f).astype(BF)
    both = jnp.stack([w_gate, w_up]).transpose(0, 2, 1, 3).reshape(-1, hidden_w)
    both = jnp.dot(both, select, preferred_element_type=F32).astype(BF)
    both = both.reshape(2, experts_n, own_d, N_C, part_f).transpose(3, 2, 0, 1, 4)
    gate_up = fetch_rows(both.reshape(N_C, own_d, 2 * spread))
    down_own = w_down.reshape(N_C, N_CHIPS, part_down * experts_n, model_w)
    down_own = lax.dynamic_index_in_dim(down_own, y_at, 1, False)
    down = fetch_rows(down_own)
    out_full = fetch_rows(jnp.broadcast_to(w_out[None], (N_C, *w_out.shape)))
    down = down.reshape(-1, experts_n, model_w).transpose(1, 0, 2).reshape(spread, model_w)

    row_ids = jnp.arange(rows, dtype=jnp.int32)
    lengths = seq_lengths[0]
    seq_ends = jnp.cumsum(lengths)
    seq_starts = seq_ends - lengths
    segment = jnp.sum((row_ids[None, :] >= seq_ends[:, None]).astype(jnp.int32), axis=0)
    in_seq = segment[None, :] == jnp.arange(lengths.shape[0], dtype=jnp.int32)[:, None]
    positions = row_ids - jnp.sum(jnp.where(in_seq, seq_starts[:, None], 0), axis=0)
    expert_ids = jnp.arange(experts_n, dtype=jnp.int32)
    routed = jnp.any(routes.T[None, :, :] == expert_ids[:, None, None], axis=1)
    aux = jnp.concatenate(
        [
            routed.astype(BF),
            positions.astype(BF)[None, :],
            segment.astype(BF)[None, :],
            jnp.zeros((2, rows), BF),
        ]
    )
    tok_all = gather_group(tokens).reshape(group_t, model_w)
    aux_all = gather_group(aux)
    cot_all = gather_group(out_cotangent).reshape(group_t, model_w)
    routed_all = aux_all[:, :experts_n].transpose(1, 0, 2).reshape(experts_n, group_t) > 0.5
    pos_all = aux_all[:, experts_n].astype(F32)
    seg_all = aux_all[:, experts_n + 1].astype(F32)
    allowed = (row_ids[None, None, :] <= row_ids[None, :, None]) & (
        seg_all[:, :, None] == seg_all[:, None, :]
    )

    half = HEAD_DIM // 2
    inverse = 10000.0 ** (-2.0 * jnp.arange(half, dtype=F32) / HEAD_DIM)
    angles = jnp.arange(MAX_LEN, dtype=F32)[:, None] * inverse[None, :]
    table = jnp.concatenate(
        [jnp.tile(jnp.cos(angles), (1, 2 * qk_w // HEAD_DIM)), jnp.tile(jnp.sin(angles), (1, 2 * qk_w // HEAD_DIM))],
        axis=1,
    )
    pos_hot = (
        pos_all.reshape(group_t)[:, None] == jnp.arange(MAX_LEN, dtype=F32)[None, :]
    ).astype(F32)
    trig = dot(pos_hot, table, 1, 0, HIGHEST)
    cosine, sine = trig[:, :qk_w], trig[:, qk_w:]
    lane = np.arange(qk_w)
    turn = np.zeros((qk_w, qk_w), np.float32)
    turn[lane // HEAD_DIM * HEAD_DIM + (lane + half) % HEAD_DIM, lane] = np.where(
        lane % HEAD_DIM < half, -1.0, 1.0
    )
    scale = HEAD_DIM ** (-0.5)
    to_scale = jnp.asarray(np.where(lane < q_w, scale, 1.0)[None, :], F32)

    gain_in = dense[:, qkv_w + out_w].astype(F32)
    gain_mid = dense[:, qkv_w + out_w + 1].astype(F32)
    router = dense[:, qkv_w + out_w + 2 : qkv_w + out_w + 2 + experts_n]
    w_qkv = dense[:, :qkv_w]
    out_part = dense[:, qkv_w : qkv_w + out_w]
    x_all = tok_all.astype(F32)
    inv_all = lax.rsqrt(jnp.mean(x_all * x_all, axis=1, keepdims=True) + EPSILON)
    normed_in = (x_all * inv_all * gain_in[None, :]).astype(BF)
    w_turn = dot(w_qkv[:, :qk_w], jnp.asarray(turn, BF), 1, 0).astype(BF)
    qkv = dot(normed_in, jnp.concatenate([w_qkv, w_turn], axis=1), 1, 0)
    rotated = ((qkv[:, :qk_w] * cosine + qkv[:, qkv_w:] * sine) * to_scale).astype(BF)
    query = [
        rotated[:, k * HEAD_DIM : (k + 1) * HEAD_DIM].reshape(N_GROUP, rows, HEAD_DIM)
        for k in range(HEADS // KV_HEADS)
    ]
    key = rotated[:, q_w:].reshape(N_GROUP, rows, HEAD_DIM)
    value = qkv[:, qk_w:qkv_w].astype(BF).reshape(N_GROUP, rows, HEAD_DIM)
    query = jnp.concatenate(query, axis=1)
    scores = jnp.einsum("bqd,bsd->bqs", query, key, preferred_element_type=F32)
    scores = scores.reshape(N_GROUP, -1, rows, rows)
    masked = jnp.where(allowed[:, None], scores, -1000000000.0)
    exps = jnp.exp(masked - jnp.max(masked, axis=-1, keepdims=True))
    probs = exps / jnp.sum(exps, axis=-1, keepdims=True)
    probs = probs.reshape(N_GROUP, -1, rows)
    probs_low = probs.astype(BF)
    attended = jnp.einsum("bqs,bsd->bqd", probs_low, value, preferred_element_type=F32)
    attended = attended.astype(BF).reshape(N_GROUP, -1, rows, HEAD_DIM)
    attended = jnp.concatenate([attended[:, k] for k in range(HEADS // KV_HEADS)], axis=-1)
    att_all = gather_group(attended.reshape(group_t, q_w))
    branch_cols = jnp.einsum(
        "qtk,qkn->tn", att_all, out_part.reshape(N_GROUP, q_w, out_w), preferred_element_type=F32
    )
    branch = swap(branch_cols.astype(BF).reshape(N_GROUP, rows, out_w), GROUP)
    branch = branch.transpose(1, 0, 2).reshape(rows, model_w)

    x_own = tokens.astype(F32)
    mixed = x_own + branch.astype(F32)
    inv_mid = lax.rsqrt(jnp.mean(mixed * mixed, axis=1, keepdims=True) + EPSILON)
    unit_mid = mixed * inv_mid
    normed_mid = (unit_mid * gain_mid[None, :]).astype(BF)
    mid_all = gather_group(normed_mid).reshape(group_t, model_w)

    def gates_of(logits, chosen):
        top = jnp.max(jnp.where(chosen, logits, -jnp.inf), axis=0, keepdims=True)
        exps = jnp.where(chosen, jnp.exp(jnp.where(chosen, logits - top, 0.0)), 0.0)
        return exps / jnp.sum(exps, axis=0, keepdims=True)

    gates_all = gates_of(dot(router, mid_all, 0, 1), routed_all)
    of_expert = np.repeat(np.eye(experts_n, dtype=np.float32), part_f, axis=1)
    gates_wide = dot(gates_all, jnp.asarray(of_expert), 0, 0, HIGHEST)
    pre = dot(mid_all, gate_up, 1, 0)
    gate_pre, up_pre = pre[:, :spread], pre[:, spread:]
    gate_sig = jax.nn.sigmoid(gate_pre)
    gate_act = gate_pre * gate_sig
    hidden = gate_act * up_pre
    hidden_gated = (hidden * gates_wide).astype(BF)
    hidden_raw = dot(cot_all, down, 1, 1)
    gate_grad = dot(jnp.asarray(of_expert), hidden.astype(BF).astype(F32) * hidden_raw, 1, 1, HIGHEST)
    hidden_grad = hidden_raw * gates_wide
    pre_grad = jnp.concatenate(
        [
            (hidden_grad * up_pre * gate_sig * (1.0 + gate_pre * (1.0 - gate_sig))).astype(BF),
            (hidden_grad * gate_act).astype(BF),
        ],
        axis=1,
    )
    gate_grad = gate_grad.reshape(experts_n, N_GROUP, rows).transpose(1, 0, 2)
    gate_grad = jnp.sum(swap(gate_grad, GROUP), axis=0)
    branch_part = dot(hidden_gated, down, 1, 0).astype(BF).reshape(N_GROUP, rows, model_w)
    grad_gu = dot(mid_all, pre_grad, 0, 0).astype(BF)
    grad_dn = dot(hidden_gated, cot_all, 0, 0).astype(BF)
    mid_part = dot(pre_grad, gate_up, 1, 1).astype(BF).reshape(N_GROUP, rows, model_w)
    mid_grad = scatter_group(mid_part, (grad_dn,), (grad_gu,))
    grad_dn = grad_dn.reshape(experts_n, part_f, model_w).transpose(1, 0, 2)
    grad_dn = grad_dn.reshape(part_f * experts_n, model_w)
    grad_gu = lax.psum_scatter(grad_gu, "z", scatter_dimension=0, tiled=True)
    grad_dn = lax.psum_scatter(grad_dn, "z", scatter_dimension=0, tiled=True)
    output = (mixed + scatter_group(branch_part)).astype(BF)

    cot = out_cotangent.astype(F32)
    gates = gates_of(dot(router, normed_mid, 0, 1), routed)
    logit_grad = gates * (gate_grad - jnp.sum(gates * gate_grad, axis=0, keepdims=True))
    mid_grad = mid_grad + dot(logit_grad, router.astype(F32), 0, 1, HIGHEST)
    scaled_mid = mid_grad * gain_mid[None, :]
    mixed_grad = cot + inv_mid * (
        scaled_mid - unit_mid * jnp.mean(scaled_mid * unit_mid, axis=1, keepdims=True)
    )
    gain_mid_term = jnp.sum(mid_grad * unit_mid, axis=0)
    router_term = dot(normed_mid.astype(F32), logit_grad, 0, 1, HIGHEST)
    mixed_low = mixed_grad.astype(BF)
    att_grad = dot(mixed_low, out_full, 1, 1).astype(BF)
    sent = jnp.stack([att_grad, mixed_low]).reshape(2, rows, N_GROUP, q_w).transpose(2, 0, 1, 3)
    sent = swap(sent, GROUP)
    att_grad = sent[:, 0]
    mixed_cols = sent[:, 1].reshape(group_t, out_w)

    att_grad = jnp.concatenate(
        [
            att_grad[:, :, k * HEAD_DIM : (k + 1) * HEAD_DIM]
            for k in range(HEADS // KV_HEADS)
        ],
        axis=1,
    )
    value_grad = jnp.einsum("bqs,bqd->bsd", probs_low, att_grad, preferred_element_type=F32)
    prob_grad = jnp.einsum("bqd,bsd->bqs", att_grad, value, preferred_element_type=F32)
    score_grad = (
        probs * (prob_grad - jnp.sum(probs * prob_grad, axis=-1, keepdims=True))
    ).astype(BF)
    query_grad = jnp.einsum("bqs,bsd->bqd", score_grad, key, preferred_element_type=F32)
    query_grad = query_grad.reshape(N_GROUP, -1, rows, HEAD_DIM)
    key_grad = jnp.einsum("bqs,bqd->bsd", score_grad, query, preferred_element_type=F32)
    turned = jnp.concatenate(
        [query_grad[:, k] for k in range(HEADS // KV_HEADS)] + [key_grad], axis=-1
    ).reshape(group_t, qk_w)
    turned = turned * to_scale
    turned = turned * cosine + dot(turned * sine, jnp.asarray(turn), 1, 1, HIGHEST)
    qkv_grad = jnp.concatenate(
        [turned.astype(BF), value_grad.astype(BF).reshape(group_t, kv_w)], axis=1
    )
    in_part = dot(qkv_grad, w_qkv, 1, 1)
    gain_in_term = jnp.sum(in_part * (x_all * inv_all), axis=0)
    grad_qkv = dot(normed_in, qkv_grad, 0, 0)
    grad_out = jnp.einsum("qtk,tn->qkn", att_all, mixed_cols, preferred_element_type=F32)
    grad_out = grad_out.reshape(model_w, out_w)
    grad_dense = jnp.concatenate(
        [
            grad_qkv.astype(BF),
            grad_out.astype(BF),
            gain_in_term.astype(BF)[:, None],
            gain_mid_term.astype(BF)[:, None],
            router_term.astype(BF),
            jnp.zeros((model_w, 128 - 2 - experts_n), BF),
        ],
        axis=1,
    )
    grad_dense = lax.psum_scatter(grad_dense, "z", scatter_dimension=0, tiled=True)
    in_grad = scatter_group(in_part.astype(BF).reshape(N_GROUP, rows, model_w))
    inv_in = lax.rsqrt(jnp.mean(x_own * x_own, axis=1, keepdims=True) + EPSILON)
    unit_in = x_own * inv_in
    scaled_in = in_grad * gain_in[None, :]
    tokens_grad = mixed_grad + inv_in * (
        scaled_in - unit_in * jnp.mean(scaled_in * unit_in, axis=1, keepdims=True)
    )

    expert_parts = jnp.concatenate(
        [
            grad_gu.reshape(N_XH, N_C, -1, 128),
            grad_dn.reshape(N_XH, N_C, -1, 128),
        ],
        axis=2,
    )
    lines = expert_parts.shape[2]
    expert_parts = to_owners(expert_parts.reshape(N_XH, N_C * lines, 128))
    gu_lines = own_d * 2 * spread // 128
    gu_all = expert_parts[:, :gu_lines].reshape(N_GROUP, own_d, 2, experts_n, part_f)
    gu_all = gu_all.transpose(2, 3, 1, 0, 4).reshape(-1, hidden_w)
    g_ids = jnp.arange(hidden_w, dtype=jnp.int32)[:, None]
    h_ids = g_ids % part_f
    place = own_f * (h_ids // part_down) + part_down * (g_ids // part_f) + h_ids % part_down
    spread_out = (place == jnp.arange(hidden_w, dtype=jnp.int32)[None, :]).astype(BF)
    gu_all = dot(gu_all, spread_out, 1, 0).reshape(2, experts_n, own_d, hidden_w)
    gu_all = gu_all.transpose(0, 2, 1, 3)
    grad_w_gate, grad_w_up = gu_all[0], gu_all[1]
    grad_w_down = expert_parts[:, gu_lines:].reshape(own_f, experts_n, model_w).astype(F32)

    dense_parts = to_owners_at_once(grad_dense.reshape(N_XH, N_C * own_d, -1))

    def side(at, width):
        return dense_parts[:, :, at : at + width].transpose(1, 0, 2).reshape(own_d, -1)

    grad_w_query = side(0, q_w)
    grad_w_key = side(q_w, kv_w)
    grad_w_value = side(qk_w, kv_w)
    grad_w_out = side(qkv_w, out_w)
    aux_grad = jnp.sum(dense_parts[:, :, qkv_w + out_w :], axis=0)
    return (
        output,
        tokens_grad,
        aux_grad[:, 0],
        grad_w_query,
        grad_w_key,
        grad_w_value,
        grad_w_out,
        aux_grad[:, 1],
        aux_grad[:, 2 : 2 + experts_n],
        grad_w_gate,
        grad_w_up,
        grad_w_down,
    )


def solution(mesh):
    split = Mesh(mesh.devices.reshape([SIZES[k] for k in REP_SHARD]), REP_SHARD)
    placed = (
        P(REP_SHARD, None),
        P(REP_SHARD, None),
        P(REP_SHARD, None),
        P(REP_SHARD, None),
        P(SHARD),
        P(SHARD, None),
        P(SHARD, None),
        P(SHARD, None),
        P(SHARD, None),
        P(SHARD),
        P(SHARD, None),
        P(SHARD, None, None),
        P(SHARD, None, None),
        P(SHARD, None, None),
    )
    return jax.shard_map(
        on_device,
        mesh=split,
        in_specs=placed,
        out_specs=(
            P(REP_SHARD, None),
            P(REP_SHARD, None),
            P(SHARD),
            P(SHARD, None),
            P(SHARD, None),
            P(SHARD, None),
            P(SHARD, None),
            P(SHARD),
            P(SHARD, None),
            P(SHARD, None, None),
            P(SHARD, None, None),
            P(SHARD, None, None),
        ),
        check_vma=False,
    )
```

```python
import jax
import jax.numpy as jnp
import numpy as np
from jax import lax
from jax.experimental import pallas as pl
from jax.experimental.pallas import tpu as pltpu
from jax.sharding import Mesh
from jax.sharding import PartitionSpec as P

HEADS = 16
KV_HEADS = 8
HEAD_DIM = 64
LANES = 128
SHARD = ("z", "xh", "c")
REP_SHARD = ("xl", "yh", "yl", "z", "xh", "c")
CHIPS = ("xl", "yl")
APART = ("yh",)
GROUP = ("c", *CHIPS)
SIZES = {"xl": 2, "yh": 2, "yl": 2, "z": 8, "xh": 2, "c": 2}
N_CHIPS = 4
N_APART = 8 // N_CHIPS
N_C, N_XH = 2, 2
N_GROUP = N_CHIPS * N_C
MAX_LEN = 64
EPSILON = 1e-06
HIGHEST = lax.Precision.HIGHEST
BF = jnp.bfloat16
F32 = jnp.float32


def dot(a, b, ca, cb, precision=None):
    return lax.dot_general(
        a, b, (((ca,), (cb,)), ((), ())), precision=precision, preferred_element_type=F32
    )


def swap(x, axes):
    return lax.all_to_all(x, axes, 0, 0, tiled=False)


def gather_chips(x):
    return swap(jnp.broadcast_to(x[None], (N_CHIPS, *x.shape)), CHIPS)


def gather_cores(x):
    x = swap(jnp.broadcast_to(x[None], (N_C, *x.shape)), "c")
    return x.reshape(N_GROUP, *x.shape[2:])


def after(x, *others):
    for other in others:
        x = x + (other[(0,) * other.ndim] * 0).astype(x.dtype)
    return x


def scatter_cores(x, *others):
    x = x.reshape(N_C, N_CHIPS, *x.shape[1:])
    return after(jnp.sum(swap(x, "c").astype(F32), axis=0), *others).astype(BF)


def scatter_chips(x, *others):
    return after(jnp.sum(swap(x, CHIPS).astype(F32), axis=0), *others)


def swap_rows(x):
    x = swap(jnp.broadcast_to(x[None], (N_XH, *x.shape)).reshape(-1, *x.shape[1:]), ("xh", "c"))
    return x.reshape(-1, x.shape[-1])


def owner_sums(x):
    x = jnp.broadcast_to(x[None], (N_APART, *x.shape))
    x = x.reshape(N_APART * N_XH, *x.shape[2:])
    return jnp.sum(swap(x, (*APART, "xh")).astype(F32), axis=0).astype(BF)


def to_owners(x):
    rows = x.shape[0] // N_C
    x = x.reshape(N_C, 1, rows, *x.shape[1:])
    x = jnp.broadcast_to(x, (N_C, N_CHIPS, *x.shape[2:])).reshape(N_GROUP, *x.shape[2:])
    return swap(x, GROUP)


def spread_sums(x):
    rows, width = x.shape[0] // (N_XH * N_C), x.shape[1]
    x = jnp.broadcast_to(
        x.reshape(1, N_XH, N_C, 1, rows, width), (N_APART, N_XH, N_C, N_CHIPS, rows, width)
    )
    x = swap(x.reshape(-1, rows, width), (*APART, "xh", *GROUP))
    return jnp.sum(x.reshape(N_APART * N_XH, N_GROUP, rows, width).astype(F32), axis=0)


def gates_of(logits, chosen):
    top = jnp.max(jnp.where(chosen, logits, -1e30), axis=1, keepdims=True)
    exps = jnp.where(chosen, jnp.exp(jnp.where(chosen, logits - top, 0.0)), 0.0)
    return exps / jnp.sum(exps, axis=1, keepdims=True)


def experts_kernel(
    experts_n, mid, cot, gate_up, down, router, marks, hot, sent, pre_grad, hidden_gated
):
    model_w, spread = mid.shape[1], down.shape[0]
    lane = lax.broadcasted_iota(jnp.int32, marks.shape, 1)
    chosen = (marks[...] > 0.5) & (lane < experts_n)
    gates = gates_of(dot(mid[...], router[...], 1, 0), chosen)
    high = gates.astype(BF)
    low = (gates - high.astype(F32)).astype(BF)
    wide = dot(high, hot[...], 1, 0) + dot(low, hot[...], 1, 0)
    gate_pre = dot(mid[...], gate_up[:, :spread], 1, 0)
    up_pre = dot(mid[...], gate_up[:, spread:], 1, 0)
    hidden_raw = dot(cot[...], down[...], 1, 1)
    sig = 1.0 / (1.0 + jnp.exp(-gate_pre))
    act = gate_pre * sig
    hidden = act * up_pre
    gated = (hidden * wide).astype(BF)
    hidden_gated[...] = gated
    products = hidden * hidden_raw
    high = products.astype(BF)
    low = (products - high.astype(F32)).astype(BF)
    gate_grad = dot(high, hot[...], 1, 1) + dot(low, hot[...], 1, 1)
    hidden_grad = hidden_raw * wide
    gate_pre_grad = (hidden_grad * up_pre * sig * (1.0 + gate_pre * (1.0 - sig))).astype(BF)
    up_pre_grad = (hidden_grad * act).astype(BF)
    pre_grad[:, :spread] = gate_pre_grad
    pre_grad[:, spread:] = up_pre_grad
    mid_part = dot(gate_pre_grad, gate_up[:, :spread], 1, 1)
    mid_part = mid_part + dot(up_pre_grad, gate_up[:, spread:], 1, 1)
    sent[:, :model_w] = mid_part.astype(BF)
    sent[:, model_w : model_w + LANES] = gate_grad.astype(BF)
    sent[:, model_w + LANES :] = dot(gated, down[...], 1, 0).astype(BF)


def experts(mid, cot, gate_up, down, router, marks, experts_n):
    tokens_n, model_w = mid.shape
    spread = down.shape[0]
    step = tokens_n // 4
    hot = np.zeros((LANES, spread), np.float32)
    hot[np.arange(spread) % experts_n, np.arange(spread)] = 1.0

    def by_rows(width):
        return pl.BlockSpec((step, width), lambda i: (i, 0))

    def whole(x):
        return pl.BlockSpec(x.shape, lambda i: (0, 0))

    hot = jnp.asarray(hot, BF)
    sent_w = 2 * model_w + LANES
    return pl.pallas_call(
        lambda *refs: experts_kernel(experts_n, *refs),
        grid=(tokens_n // step,),
        in_specs=[
            by_rows(model_w),
            by_rows(model_w),
            whole(gate_up),
            whole(down),
            whole(router),
            by_rows(LANES),
            whole(hot),
        ],
        out_specs=[by_rows(sent_w), by_rows(2 * spread), by_rows(spread)],
        out_shape=[
            jax.ShapeDtypeStruct((tokens_n, sent_w), BF),
            jax.ShapeDtypeStruct((tokens_n, 2 * spread), BF),
            jax.ShapeDtypeStruct((tokens_n, spread), BF),
        ],
        compiler_params=pltpu.CompilerParams(vmem_limit_bytes=44 * 2**20),
        cost_estimate=pl.CostEstimate(
            flops=12 * tokens_n * model_w * spread, bytes_accessed=20 * 2**20, transcendentals=0
        ),
    )(mid, cot, gate_up, down, router, marks, hot)


def on_device(
    tokens,
    out_cotangent,
    seq_lengths,
    routes,
    gain_attn,
    w_query,
    w_key,
    w_value,
    w_out,
    gain_ffn,
    w_router,
    w_gate,
    w_up,
    w_down,
):
    rows, model_w = tokens.shape
    experts_n = w_router.shape[1]
    hidden_w = w_gate.shape[2]
    own_d = w_gate.shape[0]
    group_t = rows * N_GROUP
    kv_w = HEAD_DIM
    q_w = HEADS // KV_HEADS * HEAD_DIM
    qk_w = q_w + kv_w
    qkv_w = qk_w + kv_w
    out_w = model_w // N_GROUP
    part_f = hidden_w // N_GROUP
    spread = experts_n * part_f
    own_f = w_down.shape[0]
    part_down = own_f // N_GROUP
    y_at = lax.axis_index(CHIPS)

    def columns(w, width):
        return jnp.stack(
            [
                lax.dynamic_slice_in_dim(w, (k * N_CHIPS + y_at) * width, width, axis=1)
                for k in range(N_C)
            ]
        )

    aux_w = jnp.concatenate(
        [
            w_router,
            gain_attn[:, None],
            gain_ffn[:, None],
            jnp.zeros((own_d, LANES - 2 - experts_n), BF),
        ],
        axis=1,
    )
    dense_own = jnp.concatenate(
        [
            columns(w_query, q_w),
            columns(w_key, kv_w),
            columns(w_value, kv_w),
            jnp.broadcast_to(aux_w[None], (N_C, own_d, 128)),
        ],
        axis=2,
    )
    f_ids = jnp.arange(hidden_w, dtype=jnp.int32)[:, None]
    s_ids = jnp.arange(N_C * part_f, dtype=jnp.int32)[None, :]
    k_ids = s_ids % part_f
    picked_f = (
        own_f * (k_ids // part_down)
        + part_down * (s_ids // part_f * N_CHIPS + y_at)
        + k_ids % part_down
    )
    select = (f_ids == picked_f).astype(BF)
    both = jnp.stack([w_gate, w_up]).transpose(0, 2, 1, 3).reshape(-1, hidden_w)
    both = jnp.dot(both, select, preferred_element_type=F32).astype(BF)
    both = both.reshape(2, experts_n, own_d, N_C, part_f).transpose(3, 2, 0, 1, 4)
    unit = np.arange(spread)
    interleave = np.zeros((spread, spread), np.float32)
    interleave[unit, unit % part_f * experts_n + unit // part_f] = 1.0
    interleave = jnp.asarray(interleave, BF)
    both = dot(both.reshape(-1, spread), interleave, 1, 0).astype(BF)
    both = both.reshape(N_C, own_d, 2 * spread)
    down_own = w_down.reshape(N_C, N_CHIPS, part_down * experts_n, model_w)
    down_own = lax.dynamic_index_in_dim(down_own, y_at, 1, False)
    down_own = jnp.pad(down_own, ((0, 0), (0, own_d - part_down * experts_n), (0, 0)))
    out_own = jnp.broadcast_to(w_out[None], (N_C, *w_out.shape))
    row_ids = jnp.arange(rows, dtype=jnp.int32)
    lengths = seq_lengths[0]
    seq_ends = jnp.cumsum(lengths)
    seq_starts = seq_ends - lengths
    segment = jnp.sum((row_ids[None, :] >= seq_ends[:, None]).astype(jnp.int32), axis=0)
    in_seq = segment[None, :] == jnp.arange(lengths.shape[0], dtype=jnp.int32)[:, None]
    positions = row_ids - jnp.sum(jnp.where(in_seq, seq_starts[:, None], 0), axis=0)
    expert_ids = jnp.arange(experts_n, dtype=jnp.int32)
    routed = jnp.any(routes[:, :, None] == expert_ids[None, None, :], axis=1)
    aux = jnp.concatenate(
        [
            routed.astype(BF),
            positions.astype(BF)[:, None],
            segment.astype(BF)[:, None],
            jnp.zeros((rows, LANES - 2 - experts_n), BF),
        ],
        axis=1,
    )
    tok_chips = gather_chips(jnp.concatenate([tokens, aux], axis=1))
    tok_all = gather_cores(tok_chips)
    aux_all = tok_all[:, :, model_w:]
    tok_all = tok_all.reshape(group_t, -1)[:, :model_w]
    cot_chips = gather_chips(out_cotangent)
    first_own = swap_rows(jnp.concatenate([dense_own, out_own], axis=2))
    second_own = swap_rows(after(jnp.concatenate([both, down_own], axis=2), tok_chips))
    first = lax.all_gather(first_own, "z", axis=0, tiled=True)
    second = lax.all_gather(second_own, "z", axis=0, tiled=True)
    dense, out_full = first[:, : qkv_w + 128], first[:, qkv_w + 128 :]
    gate_up, down = second[:, : 2 * spread], second[:, 2 * spread :]
    down = down.reshape(-1, own_d, model_w)[:, : part_down * experts_n].reshape(spread, model_w)
    pos_all = aux_all[:, :, experts_n].astype(F32)
    seg_all = aux_all[:, :, experts_n + 1].astype(F32)
    allowed = (row_ids[None, None, :] <= row_ids[None, :, None]) & (
        seg_all[:, :, None] == seg_all[:, None, :]
    )

    half = HEAD_DIM // 2
    inverse = 10000.0 ** (-2.0 * jnp.arange(half, dtype=F32) / HEAD_DIM)
    angles = jnp.arange(MAX_LEN, dtype=F32)[:, None] * inverse[None, :]
    table = jnp.concatenate(
        [jnp.tile(jnp.cos(angles), (1, 2 * qk_w // HEAD_DIM)), jnp.tile(jnp.sin(angles), (1, 2 * qk_w // HEAD_DIM))],
        axis=1,
    )
    pos_hot = (
        pos_all.reshape(group_t)[:, None] == jnp.arange(MAX_LEN, dtype=F32)[None, :]
    ).astype(F32)
    trig = dot(pos_hot, table, 1, 0, HIGHEST)
    cosine, sine = trig[:, :qk_w], trig[:, qk_w:]
    lane = np.arange(qk_w)
    turn = np.zeros((qk_w, qk_w), np.float32)
    turn[lane // HEAD_DIM * HEAD_DIM + (lane + half) % HEAD_DIM, lane] = np.where(
        lane % HEAD_DIM < half, -1.0, 1.0
    )
    scale = HEAD_DIM ** (-0.5)
    to_scale = jnp.asarray(np.where(lane < q_w, scale, 1.0)[None, :], F32)

    aux_full = dense[:, qkv_w:]
    gain_in = aux_full[:, experts_n].astype(F32)
    gain_mid = aux_full[:, experts_n + 1].astype(F32)
    router = aux_full[:, :experts_n]
    w_qkv = dense[:, :qkv_w]
    x_all = tok_all.astype(F32)
    inv_all = lax.rsqrt(jnp.mean(x_all * x_all, axis=1, keepdims=True) + EPSILON)
    normed_in = (x_all * inv_all * gain_in[None, :]).astype(BF)
    w_turn = dot(w_qkv[:, :qk_w], jnp.asarray(turn, BF), 1, 0).astype(BF)
    qkv = dot(normed_in, jnp.concatenate([w_qkv, w_turn], axis=1), 1, 0)
    rotated = ((qkv[:, :qk_w] * cosine + qkv[:, qkv_w:] * sine) * to_scale).astype(BF)
    query = [
        rotated[:, k * HEAD_DIM : (k + 1) * HEAD_DIM].reshape(N_GROUP, rows, HEAD_DIM)
        for k in range(HEADS // KV_HEADS)
    ]
    key = rotated[:, q_w:].reshape(N_GROUP, rows, HEAD_DIM)
    value = qkv[:, qk_w:qkv_w].astype(BF).reshape(N_GROUP, rows, HEAD_DIM)
    query = jnp.concatenate(query, axis=1)
    scores = jnp.einsum("bqd,bsd->bqs", query, key, preferred_element_type=F32)
    scores = scores.reshape(N_GROUP, -1, rows, rows)
    masked = jnp.where(allowed[:, None], scores, -1000000000.0)
    exps = jnp.exp(masked - jnp.max(masked, axis=-1, keepdims=True))
    probs = exps / jnp.sum(exps, axis=-1, keepdims=True)
    probs = probs.reshape(N_GROUP, -1, rows)
    probs_low = probs.astype(BF)
    attended = jnp.einsum("bqs,bsd->bqd", probs_low, value, preferred_element_type=F32)
    attended = attended.astype(BF).reshape(N_GROUP, -1, rows, HEAD_DIM)
    attended = jnp.concatenate([attended[:, k] for k in range(HEADS // KV_HEADS)], axis=-1)
    attended = attended.reshape(N_GROUP, rows, q_w)
    att_own = swap(attended, GROUP).transpose(1, 0, 2).reshape(rows, model_w)

    x_own = tokens.astype(F32)
    mixed = x_own + dot(att_own, out_full, 1, 0)
    inv_mid = lax.rsqrt(jnp.mean(mixed * mixed, axis=1, keepdims=True) + EPSILON)
    unit_mid = mixed * inv_mid
    normed_mid = (unit_mid * gain_mid[None, :]).astype(BF)
    cot_all = gather_cores(cot_chips).reshape(group_t, model_w)
    mid_all = gather_cores(gather_chips(normed_mid)).reshape(group_t, model_w)
    att_chips = gather_chips(attended.reshape(group_t, q_w))
    att_all = gather_cores(att_chips)

    sent, pre_grad, hidden_gated = experts(
        mid_all, cot_all, gate_up, down, aux_full, aux_all.reshape(group_t, LANES), experts_n
    )
    grad_gu = dot(mid_all, pre_grad, 0, 0).astype(BF)
    grad_dn = dot(hidden_gated, cot_all, 0, 0).astype(BF)
    back = scatter_cores(sent.reshape(N_GROUP, rows, -1), grad_dn)
    back = scatter_chips(back, grad_gu)
    mid_grad, gate_grad = back[:, :model_w], back[:, model_w : model_w + experts_n]
    output = (mixed + back[:, model_w + LANES :]).astype(BF)
    grad_gu = lax.psum_scatter(grad_gu, "z", scatter_dimension=0, tiled=True)
    grad_dn = lax.psum_scatter(grad_dn, "z", scatter_dimension=0, tiled=True)
    cot = out_cotangent.astype(F32)
    gates = gates_of(dot(normed_mid, router, 1, 0), routed)
    logit_grad = gates * (gate_grad - jnp.sum(gates * gate_grad, axis=1, keepdims=True))
    mid_grad = mid_grad + dot(logit_grad, router.astype(F32), 1, 1, HIGHEST)
    scaled_mid = mid_grad * gain_mid[None, :]
    mixed_grad = cot + inv_mid * (
        scaled_mid - unit_mid * jnp.mean(scaled_mid * unit_mid, axis=1, keepdims=True)
    )
    gain_mid_term = jnp.sum(mid_grad * unit_mid, axis=0)
    router_term = dot(normed_mid.astype(F32), logit_grad, 0, 0, HIGHEST)
    mixed_low = mixed_grad.astype(BF)
    att_grad = dot(mixed_low, out_full, 1, 1).astype(BF)
    sent = jnp.stack([att_grad, mixed_low]).reshape(2, rows, N_GROUP, q_w).transpose(2, 0, 1, 3)
    sent = swap(sent, GROUP)
    att_grad = sent[:, 0]
    mixed_cols = sent[:, 1].reshape(group_t, out_w)

    att_grad = jnp.concatenate(
        [
            att_grad[:, :, k * HEAD_DIM : (k + 1) * HEAD_DIM]
            for k in range(HEADS // KV_HEADS)
        ],
        axis=1,
    )
    value_grad = jnp.einsum("bqs,bqd->bsd", probs_low, att_grad, preferred_element_type=F32)
    prob_grad = jnp.einsum("bqd,bsd->bqs", att_grad, value, preferred_element_type=F32)
    score_grad = (
        probs * (prob_grad - jnp.sum(probs * prob_grad, axis=-1, keepdims=True))
    ).astype(BF)
    query_grad = jnp.einsum("bqs,bsd->bqd", score_grad, key, preferred_element_type=F32)
    query_grad = query_grad.reshape(N_GROUP, -1, rows, HEAD_DIM)
    key_grad = jnp.einsum("bqs,bqd->bsd", score_grad, query, preferred_element_type=F32)
    turned = jnp.concatenate(
        [query_grad[:, k] for k in range(HEADS // KV_HEADS)] + [key_grad], axis=-1
    ).reshape(group_t, qk_w)
    turned = turned * to_scale
    turned = turned * cosine + dot(turned * sine, jnp.asarray(turn), 1, 1, HIGHEST)
    qkv_grad = jnp.concatenate(
        [turned.astype(BF), value_grad.astype(BF).reshape(group_t, kv_w)], axis=1
    )
    in_part = dot(qkv_grad, w_qkv, 1, 1)
    gain_in_term = jnp.sum(in_part * (x_all * inv_all), axis=0)
    grad_qkv = dot(normed_in, qkv_grad, 0, 0)
    grad_out = jnp.einsum("qtk,tn->qkn", att_all, mixed_cols, preferred_element_type=F32)
    grad_out = grad_out.reshape(model_w, out_w)
    grad_dense = jnp.concatenate(
        [
            grad_qkv.astype(BF),
            grad_out.astype(BF),
            router_term.astype(BF),
            gain_in_term.astype(BF)[:, None],
            gain_mid_term.astype(BF)[:, None],
            jnp.zeros((model_w, LANES - 2 - experts_n), BF),
        ],
        axis=1,
    )
    pair_w = 2 * part_f
    col = np.arange(2 * spread)
    pairing = np.zeros((2 * spread, 2 * spread), np.float32)
    pairing[
        col, col % experts_n * pair_w + col // spread * part_f + col % spread // experts_n
    ] = 1.0
    grad_gu = dot(grad_gu, jnp.asarray(pairing, BF), 1, 0).astype(BF)
    grad_gu = grad_gu.reshape(N_XH * N_C, own_d, experts_n, pair_w).transpose(0, 2, 1, 3)
    parts = jnp.concatenate(
        [
            grad_gu.reshape(N_XH, N_C, experts_n * own_d, pair_w),
            grad_dn.reshape(N_XH, N_C, -1, LANES),
        ],
        axis=2,
    )
    parts = to_owners(owner_sums(parts.reshape(N_XH, -1, LANES)))
    in_grad = scatter_chips(scatter_cores(in_part.astype(BF).reshape(N_GROUP, rows, model_w)))
    grad_dense = lax.psum_scatter(grad_dense, "z", scatter_dimension=0, tiled=True)
    dense_parts = spread_sums(grad_dense)
    inv_in = lax.rsqrt(jnp.mean(x_own * x_own, axis=1, keepdims=True) + EPSILON)
    unit_in = x_own * inv_in
    scaled_in = in_grad * gain_in[None, :]
    tokens_grad = mixed_grad + inv_in * (
        scaled_in - unit_in * jnp.mean(scaled_in * unit_in, axis=1, keepdims=True)
    )

    gu_lines = experts_n * own_d
    g_ids = jnp.arange(N_GROUP * part_f, dtype=jnp.int32)[:, None]
    h_ids = g_ids % part_f
    place = own_f * (h_ids // part_down) + part_down * (g_ids // part_f) + h_ids % part_down
    spread_out = (place == jnp.arange(hidden_w, dtype=jnp.int32)[None, :]).astype(BF)
    pairs = parts[:, :gu_lines].reshape(N_GROUP, gu_lines, 2, part_f)

    def side_gu(k):
        x = pairs[:, :, k].transpose(1, 0, 2).reshape(gu_lines, N_GROUP * part_f)
        x = dot(x, spread_out, 1, 0)
        return x.reshape(experts_n, own_d, hidden_w).transpose(1, 0, 2)

    grad_w_gate, grad_w_up = side_gu(0), side_gu(1)
    grad_w_down = parts[:, gu_lines:].astype(F32)
    grad_w_down = grad_w_down.reshape(own_f, experts_n, model_w)

    def side(at, width):
        return dense_parts[:, :, at : at + width].transpose(1, 0, 2).reshape(own_d, -1)

    grad_w_query = side(0, q_w)
    grad_w_key = side(q_w, kv_w)
    grad_w_value = side(qk_w, kv_w)
    grad_w_out = side(qkv_w, out_w)
    aux_grad = jnp.sum(dense_parts[:, :, qkv_w + out_w :], axis=0)
    return (
        output,
        tokens_grad,
        aux_grad[:, experts_n],
        grad_w_query,
        grad_w_key,
        grad_w_value,
        grad_w_out,
        aux_grad[:, experts_n + 1],
        aux_grad[:, :experts_n],
        grad_w_gate,
        grad_w_up,
        grad_w_down,
    )


def solution(mesh):
    split = Mesh(mesh.devices.reshape([SIZES[k] for k in REP_SHARD]), REP_SHARD)
    placed = (
        P(REP_SHARD, None),
        P(REP_SHARD, None),
        P(REP_SHARD, None),
        P(REP_SHARD, None),
        P(SHARD),
        P(SHARD, None),
        P(SHARD, None),
        P(SHARD, None),
        P(SHARD, None),
        P(SHARD),
        P(SHARD, None),
        P(SHARD, None, None),
        P(SHARD, None, None),
        P(SHARD, None, None),
    )
    return jax.shard_map(
        on_device,
        mesh=split,
        in_specs=placed,
        out_specs=(
            P(REP_SHARD, None),
            P(REP_SHARD, None),
            P(SHARD),
            P(SHARD, None),
            P(SHARD, None),
            P(SHARD, None),
            P(SHARD, None),
            P(SHARD),
            P(SHARD, None),
            P(SHARD, None, None),
            P(SHARD, None, None),
            P(SHARD, None, None),
        ),
        check_vma=False,
    )
```

```python
import jax
import jax.numpy as jnp
import numpy as np
from jax import lax
from jax.experimental import pallas as pl
from jax.experimental.pallas import tpu as pltpu
from jax.sharding import Mesh
from jax.sharding import PartitionSpec as P

HEADS = 16
KV_HEADS = 8
HEAD_DIM = 64
LANES = 128
SHARD = ("z", "xh", "c")
REP_SHARD = ("xl", "yh", "yl", "z", "xh", "c")
CHIPS = ("xl", "yl")
APART = ("yh",)
GROUP = ("c", *CHIPS)
SIZES = {"xl": 2, "yh": 2, "yl": 2, "z": 8, "xh": 2, "c": 2}
N_CHIPS = 4
N_APART = 8 // N_CHIPS
N_C, N_XH = 2, 2
N_GROUP = N_CHIPS * N_C
MAX_LEN = 64
EPSILON = 1e-06
HIGHEST = lax.Precision.HIGHEST
BF = jnp.bfloat16
F32 = jnp.float32


def dot(a, b, ca, cb, precision=None):
    return lax.dot_general(
        a, b, (((ca,), (cb,)), ((), ())), precision=precision, preferred_element_type=F32
    )


def swap(x, axes):
    return lax.all_to_all(x, axes, 0, 0, tiled=False)


def crossed(x, axes, offset):
    n = int(np.prod([SIZES[k] for k in axes]))
    return lax.ppermute(x, axes, [(i, i ^ offset) for i in range(n)])


def gather_chips(x):
    return jnp.stack([x] + [crossed(x, CHIPS, k) for k in range(1, N_CHIPS)])


def gather_cores(x):
    return jnp.concatenate([x, crossed(x, ("c",), 1)])


def by_place(x):
    shape = x.shape
    x = x.reshape(*[SIZES[k] for k in GROUP], *shape[1:])
    for at, name in enumerate(GROUP):
        x = jnp.where(lax.axis_index(name) == 1, jnp.flip(x, at), x)
    return x.reshape(shape)


def after(x, *others):
    for other in others:
        x = x + (other[(0,) * other.ndim] * 0).astype(x.dtype)
    return x


def scatter_cores(x, *others):
    got = crossed(x[N_CHIPS:], ("c",), 1)
    return after(x[:N_CHIPS].astype(F32) + got.astype(F32), *others).astype(BF)


def scatter_chips(x, *others):
    total = x[0].astype(F32)
    for k in range(1, N_CHIPS):
        total = total + crossed(x[k], CHIPS, k).astype(F32)
    return after(total, *others)


def swap_rows(x):
    x = swap(jnp.broadcast_to(x[None], (N_XH, *x.shape)).reshape(-1, *x.shape[1:]), ("xh", "c"))
    return x.reshape(-1, x.shape[-1])


def owner_sums(x):
    x = jnp.broadcast_to(x[None], (N_APART, *x.shape))
    x = x.reshape(N_APART * N_XH, *x.shape[2:])
    return jnp.sum(swap(x, (*APART, "xh")).astype(F32), axis=0).astype(BF)


def to_owners(x):
    rows = x.shape[0] // N_C
    x = x.reshape(N_C, 1, rows, *x.shape[1:])
    x = jnp.broadcast_to(x, (N_C, N_CHIPS, *x.shape[2:])).reshape(N_GROUP, *x.shape[2:])
    return swap(x, GROUP)


def spread_sums(x):
    rows, width = x.shape[0] // (N_XH * N_C), x.shape[1]
    x = jnp.broadcast_to(
        x.reshape(1, N_XH, N_C, 1, rows, width), (N_APART, N_XH, N_C, N_CHIPS, rows, width)
    )
    x = swap(x.reshape(-1, rows, width), (*APART, "xh", *GROUP))
    return jnp.sum(x.reshape(N_APART * N_XH, N_GROUP, rows, width).astype(F32), axis=0)


def gates_of(logits, chosen):
    top = jnp.max(jnp.where(chosen, logits, -1e30), axis=1, keepdims=True)
    exps = jnp.where(chosen, jnp.exp(jnp.where(chosen, logits - top, 0.0)), 0.0)
    return exps / jnp.sum(exps, axis=1, keepdims=True)


def experts_kernel(
    experts_n, mid, cot, gate_up, down, router, marks, hot, here, there, pre_grad, hidden_gated
):
    model_w, spread = mid.shape[1], down.shape[0]
    lane = lax.broadcasted_iota(jnp.int32, marks.shape, 1)
    chosen = (marks[...] > 0.5) & (lane < experts_n)
    gates = gates_of(dot(mid[...], router[...], 1, 0), chosen)
    high = gates.astype(BF)
    low = (gates - high.astype(F32)).astype(BF)
    wide = dot(high, hot[...], 1, 0) + dot(low, hot[...], 1, 0)
    gate_pre = dot(mid[...], gate_up[:, :spread], 1, 0)
    up_pre = dot(mid[...], gate_up[:, spread:], 1, 0)
    hidden_raw = dot(cot[...], down[...], 1, 1)
    sig = 1.0 / (1.0 + jnp.exp(-gate_pre))
    act = gate_pre * sig
    hidden = act * up_pre
    gated = (hidden * wide).astype(BF)
    hidden_gated[...] = gated
    products = hidden * hidden_raw
    high = products.astype(BF)
    low = (products - high.astype(F32)).astype(BF)
    gate_grad = dot(high, hot[...], 1, 1) + dot(low, hot[...], 1, 1)
    hidden_grad = hidden_raw * wide
    gate_pre_grad = (hidden_grad * up_pre * sig * (1.0 + gate_pre * (1.0 - sig))).astype(BF)
    up_pre_grad = (hidden_grad * act).astype(BF)
    pre_grad[:, :spread] = gate_pre_grad
    pre_grad[:, spread:] = up_pre_grad
    mid_part = dot(gate_pre_grad, gate_up[:, :spread], 1, 1)
    mid_part = mid_part + dot(up_pre_grad, gate_up[:, spread:], 1, 1)
    branch = dot(gated, down[...], 1, 0)

    def store(sent):
        sent[:, :model_w] = mid_part.astype(BF)
        sent[:, model_w : model_w + LANES] = gate_grad.astype(BF)
        sent[:, model_w + LANES :] = branch.astype(BF)

    first_half = pl.program_id(0) < pl.num_programs(0) // 2
    pl.when(first_half)(lambda: store(here))
    pl.when(jnp.logical_not(first_half))(lambda: store(there))


def experts(mid, cot, gate_up, down, router, marks, experts_n):
    tokens_n, model_w = mid.shape
    spread = down.shape[0]
    steps = 4
    step = tokens_n // steps
    hot = np.zeros((LANES, spread), np.float32)
    hot[np.arange(spread) % experts_n, np.arange(spread)] = 1.0

    def by_rows(width):
        return pl.BlockSpec((step, width), lambda i: (i, 0))

    def whole(x):
        return pl.BlockSpec(x.shape, lambda i: (0, 0))

    hot = jnp.asarray(hot, BF)
    sent_w = 2 * model_w + LANES
    return pl.pallas_call(
        lambda *refs: experts_kernel(experts_n, *refs),
        grid=(tokens_n // step,),
        in_specs=[
            by_rows(model_w),
            by_rows(model_w),
            pl.BlockSpec((model_w, 2 * spread), lambda i: (0, 0)),
            whole(down),
            whole(router),
            by_rows(LANES),
            whole(hot),
        ],
        out_specs=[
            pl.BlockSpec((step, sent_w), lambda i: (jnp.minimum(i, steps // 2 - 1), 0)),
            pl.BlockSpec((step, sent_w), lambda i: (jnp.maximum(i - steps // 2, 0), 0)),
            by_rows(2 * spread),
            by_rows(spread),
        ],
        out_shape=[
            jax.ShapeDtypeStruct((tokens_n // 2, sent_w), BF),
            jax.ShapeDtypeStruct((tokens_n // 2, sent_w), BF),
            jax.ShapeDtypeStruct((tokens_n, 2 * spread), BF),
            jax.ShapeDtypeStruct((tokens_n, spread), BF),
        ],
        compiler_params=pltpu.CompilerParams(vmem_limit_bytes=44 * 2**20),
        cost_estimate=pl.CostEstimate(
            flops=12 * tokens_n * model_w * spread, bytes_accessed=20 * 2**20, transcendentals=0
        ),
    )(mid, cot, gate_up, down, router, marks, hot)


def on_device(
    tokens,
    out_cotangent,
    seq_lengths,
    routes,
    gain_attn,
    w_query,
    w_key,
    w_value,
    w_out,
    gain_ffn,
    w_router,
    w_gate,
    w_up,
    w_down,
):
    rows, model_w = tokens.shape
    experts_n = w_router.shape[1]
    hidden_w = w_gate.shape[2]
    own_d = w_gate.shape[0]
    group_t = rows * N_GROUP
    kv_w = HEAD_DIM
    q_w = HEADS // KV_HEADS * HEAD_DIM
    qk_w = q_w + kv_w
    qkv_w = qk_w + kv_w
    out_w = model_w // N_GROUP
    part_f = hidden_w // N_GROUP
    spread = experts_n * part_f
    own_f = w_down.shape[0]
    part_down = own_f // N_GROUP
    y_at = lax.axis_index(CHIPS)

    def columns(w, width):
        return jnp.stack(
            [
                lax.dynamic_slice_in_dim(w, (k * N_CHIPS + y_at) * width, width, axis=1)
                for k in range(N_C)
            ]
        )

    aux_w = jnp.concatenate(
        [
            w_router,
            gain_attn[:, None],
            gain_ffn[:, None],
            jnp.zeros((own_d, LANES - 2 - experts_n), BF),
        ],
        axis=1,
    )
    dense_own = jnp.concatenate(
        [
            columns(w_query, q_w),
            columns(w_key, kv_w),
            columns(w_value, kv_w),
            jnp.broadcast_to(aux_w[None], (N_C, own_d, 128)),
        ],
        axis=2,
    )
    f_ids = jnp.arange(hidden_w, dtype=jnp.int32)[:, None]
    s_ids = jnp.arange(N_C * part_f, dtype=jnp.int32)[None, :]
    k_ids = s_ids % part_f
    picked_f = (
        own_f * (k_ids // part_down)
        + part_down * (s_ids // part_f * N_CHIPS + y_at)
        + k_ids % part_down
    )
    select = (f_ids == picked_f).astype(BF)
    both = jnp.stack([w_gate, w_up]).transpose(0, 2, 1, 3).reshape(-1, hidden_w)
    both = jnp.dot(both, select, preferred_element_type=F32).astype(BF)
    both = both.reshape(2, experts_n, own_d, N_C, part_f).transpose(3, 2, 0, 1, 4)
    unit = np.arange(spread)
    interleave = np.zeros((spread, spread), np.float32)
    interleave[unit, unit % part_f * experts_n + unit // part_f] = 1.0
    interleave = jnp.asarray(interleave, BF)
    both = dot(both.reshape(-1, spread), interleave, 1, 0).astype(BF)
    both = both.reshape(N_C, own_d, 2 * spread)
    down_own = w_down.reshape(N_C, N_CHIPS, part_down * experts_n, model_w)
    down_own = lax.dynamic_index_in_dim(down_own, y_at, 1, False)
    down_own = jnp.pad(down_own, ((0, 0), (0, own_d - part_down * experts_n), (0, 0)))
    out_own = jnp.broadcast_to(w_out[None], (N_C, *w_out.shape))
    row_ids = jnp.arange(rows, dtype=jnp.int32)
    lengths = seq_lengths[0]
    seq_ends = jnp.cumsum(lengths)
    seq_starts = seq_ends - lengths
    segment = jnp.sum((row_ids[None, :] >= seq_ends[:, None]).astype(jnp.int32), axis=0)
    in_seq = segment[None, :] == jnp.arange(lengths.shape[0], dtype=jnp.int32)[:, None]
    positions = row_ids - jnp.sum(jnp.where(in_seq, seq_starts[:, None], 0), axis=0)
    expert_ids = jnp.arange(experts_n, dtype=jnp.int32)
    routed = jnp.any(routes[:, :, None] == expert_ids[None, None, :], axis=1)
    aux = jnp.concatenate(
        [
            routed.astype(BF),
            positions.astype(BF)[:, None],
            segment.astype(BF)[:, None],
            jnp.zeros((rows, LANES - 2 - experts_n), BF),
        ],
        axis=1,
    )
    tok_chips = gather_chips(jnp.concatenate([tokens, aux], axis=1))
    tok_all = gather_cores(tok_chips)
    aux_all = tok_all[:, :, model_w:]
    tok_all = tok_all.reshape(group_t, -1)[:, :model_w]
    cot_chips = gather_chips(out_cotangent)
    first_own = swap_rows(jnp.concatenate([dense_own, out_own], axis=2))
    second_own = swap_rows(after(jnp.concatenate([both, down_own], axis=2), tok_chips))
    first = lax.all_gather(first_own, "z", axis=0, tiled=True)
    second = lax.all_gather(second_own, "z", axis=0, tiled=True)
    dense, out_full = first[:, : qkv_w + 128], first[:, qkv_w + 128 :]
    down = second[:, 2 * spread :]
    down = down.reshape(-1, own_d, model_w)[:, : part_down * experts_n].reshape(spread, model_w)
    pos_all = aux_all[:, :, experts_n].astype(F32)
    seg_all = aux_all[:, :, experts_n + 1].astype(F32)
    allowed = (row_ids[None, None, :] <= row_ids[None, :, None]) & (
        seg_all[:, :, None] == seg_all[:, None, :]
    )

    half = HEAD_DIM // 2
    inverse = 10000.0 ** (-2.0 * jnp.arange(half, dtype=F32) / HEAD_DIM)
    angles = jnp.arange(MAX_LEN, dtype=F32)[:, None] * inverse[None, :]
    table = jnp.concatenate(
        [jnp.tile(jnp.cos(angles), (1, 2 * qk_w // HEAD_DIM)), jnp.tile(jnp.sin(angles), (1, 2 * qk_w // HEAD_DIM))],
        axis=1,
    )
    pos_hot = (
        pos_all.reshape(group_t)[:, None] == jnp.arange(MAX_LEN, dtype=F32)[None, :]
    ).astype(F32)
    trig = dot(pos_hot, table, 1, 0, HIGHEST)
    cosine, sine = trig[:, :qk_w], trig[:, qk_w:]
    lane = np.arange(qk_w)
    turn = np.zeros((qk_w, qk_w), np.float32)
    turn[lane // HEAD_DIM * HEAD_DIM + (lane + half) % HEAD_DIM, lane] = np.where(
        lane % HEAD_DIM < half, -1.0, 1.0
    )
    scale = HEAD_DIM ** (-0.5)
    to_scale = jnp.asarray(np.where(lane < q_w, scale, 1.0)[None, :], F32)

    aux_full = dense[:, qkv_w:]
    gain_in = aux_full[:, experts_n].astype(F32)
    gain_mid = aux_full[:, experts_n + 1].astype(F32)
    router = aux_full[:, :experts_n]
    w_qkv = dense[:, :qkv_w]
    x_all = tok_all.astype(F32)
    inv_all = lax.rsqrt(jnp.mean(x_all * x_all, axis=1, keepdims=True) + EPSILON)
    normed_in = (x_all * inv_all * gain_in[None, :]).astype(BF)
    w_turn = dot(w_qkv[:, :qk_w], jnp.asarray(turn, BF), 1, 0).astype(BF)
    qkv = dot(normed_in, jnp.concatenate([w_qkv, w_turn], axis=1), 1, 0)
    rotated = ((qkv[:, :qk_w] * cosine + qkv[:, qkv_w:] * sine) * to_scale).astype(BF)
    query = [
        rotated[:, k * HEAD_DIM : (k + 1) * HEAD_DIM].reshape(N_GROUP, rows, HEAD_DIM)
        for k in range(HEADS // KV_HEADS)
    ]
    key = rotated[:, q_w:].reshape(N_GROUP, rows, HEAD_DIM)
    value = qkv[:, qk_w:qkv_w].astype(BF).reshape(N_GROUP, rows, HEAD_DIM)
    query = jnp.concatenate(query, axis=1)
    scores = jnp.einsum("bqd,bsd->bqs", query, key, preferred_element_type=F32)
    scores = scores.reshape(N_GROUP, -1, rows, rows)
    masked = jnp.where(allowed[:, None], scores, -1000000000.0)
    exps = jnp.exp(masked - jnp.max(masked, axis=-1, keepdims=True))
    probs = exps / jnp.sum(exps, axis=-1, keepdims=True)
    probs = probs.reshape(N_GROUP, -1, rows)
    probs_low = probs.astype(BF)
    attended = jnp.einsum("bqs,bsd->bqd", probs_low, value, preferred_element_type=F32)
    attended = attended.astype(BF).reshape(N_GROUP, -1, rows, HEAD_DIM)
    attended = jnp.concatenate([attended[:, k] for k in range(HEADS // KV_HEADS)], axis=-1)
    attended = attended.reshape(N_GROUP, rows, q_w)
    attended = by_place(attended)
    att_own = swap(attended, GROUP).transpose(1, 0, 2).reshape(rows, model_w)

    x_own = tokens.astype(F32)
    mixed = x_own + dot(att_own, out_full, 1, 0)
    inv_mid = lax.rsqrt(jnp.mean(mixed * mixed, axis=1, keepdims=True) + EPSILON)
    unit_mid = mixed * inv_mid
    normed_mid = (unit_mid * gain_mid[None, :]).astype(BF)
    cot_all = gather_cores(cot_chips).reshape(group_t, model_w)
    mid_all = gather_cores(gather_chips(normed_mid)).reshape(group_t, model_w)
    att_chips = gather_chips(attended.reshape(group_t, q_w))
    att_all = gather_cores(att_chips)

    marks = aux_all.reshape(group_t, LANES)
    sent_here, sent_there, pre_grad, hidden_gated = experts(
        mid_all, cot_all, second, down, aux_full, marks, experts_n
    )
    grad_gu = dot(mid_all, pre_grad, 0, 0).astype(BF)
    grad_dn = dot(hidden_gated, cot_all, 0, 0).astype(BF)
    got = crossed(sent_there, ("c",), 1).reshape(N_CHIPS, rows, -1).astype(F32)
    got = after(got + sent_here.reshape(N_CHIPS, rows, -1).astype(F32), grad_dn)
    back = scatter_chips(got.astype(BF), grad_gu)
    mid_grad, gate_grad = back[:, :model_w], back[:, model_w : model_w + experts_n]
    output = (mixed + back[:, model_w + LANES :]).astype(BF)
    grad_gu = lax.psum_scatter(grad_gu, "z", scatter_dimension=0, tiled=True)
    grad_dn = lax.psum_scatter(grad_dn, "z", scatter_dimension=0, tiled=True)
    cot = out_cotangent.astype(F32)
    gates = gates_of(dot(normed_mid, router, 1, 0), routed)
    logit_grad = gates * (gate_grad - jnp.sum(gates * gate_grad, axis=1, keepdims=True))
    mid_grad = mid_grad + dot(logit_grad, router.astype(F32), 1, 1, HIGHEST)
    scaled_mid = mid_grad * gain_mid[None, :]
    mixed_grad = cot + inv_mid * (
        scaled_mid - unit_mid * jnp.mean(scaled_mid * unit_mid, axis=1, keepdims=True)
    )
    gain_mid_term = jnp.sum(mid_grad * unit_mid, axis=0)
    router_term = dot(normed_mid.astype(F32), logit_grad, 0, 0, HIGHEST)
    mixed_low = mixed_grad.astype(BF)
    att_grad = dot(mixed_low, out_full, 1, 1).astype(BF)
    sent = jnp.stack([att_grad, mixed_low]).reshape(2, rows, N_GROUP, q_w).transpose(2, 0, 1, 3)
    sent = swap(sent, GROUP)
    att_grad = by_place(sent[:, 0])
    mixed_cols = sent[:, 1].reshape(group_t, out_w)

    att_grad = jnp.concatenate(
        [
            att_grad[:, :, k * HEAD_DIM : (k + 1) * HEAD_DIM]
            for k in range(HEADS // KV_HEADS)
        ],
        axis=1,
    )
    value_grad = jnp.einsum("bqs,bqd->bsd", probs_low, att_grad, preferred_element_type=F32)
    prob_grad = jnp.einsum("bqd,bsd->bqs", att_grad, value, preferred_element_type=F32)
    score_grad = (
        probs * (prob_grad - jnp.sum(probs * prob_grad, axis=-1, keepdims=True))
    ).astype(BF)
    query_grad = jnp.einsum("bqs,bsd->bqd", score_grad, key, preferred_element_type=F32)
    query_grad = query_grad.reshape(N_GROUP, -1, rows, HEAD_DIM)
    key_grad = jnp.einsum("bqs,bqd->bsd", score_grad, query, preferred_element_type=F32)
    turned = jnp.concatenate(
        [query_grad[:, k] for k in range(HEADS // KV_HEADS)] + [key_grad], axis=-1
    ).reshape(group_t, qk_w)
    turned = turned * to_scale
    turned = turned * cosine + dot(turned * sine, jnp.asarray(turn), 1, 1, HIGHEST)
    qkv_grad = jnp.concatenate(
        [turned.astype(BF), value_grad.astype(BF).reshape(group_t, kv_w)], axis=1
    )
    in_part = dot(qkv_grad, w_qkv, 1, 1)
    gain_in_term = jnp.sum(in_part * (x_all * inv_all), axis=0)
    grad_qkv = dot(normed_in, qkv_grad, 0, 0)
    grad_out = jnp.einsum("qtk,tn->qkn", att_all, mixed_cols, preferred_element_type=F32)
    grad_out = by_place(grad_out.astype(BF)).reshape(model_w, out_w)
    grad_dense = jnp.concatenate(
        [
            grad_qkv.astype(BF),
            grad_out,
            router_term.astype(BF),
            gain_in_term.astype(BF)[:, None],
            gain_mid_term.astype(BF)[:, None],
            jnp.zeros((model_w, LANES - 2 - experts_n), BF),
        ],
        axis=1,
    )
    pair_w = 2 * part_f
    col = np.arange(2 * spread)
    pairing = np.zeros((2 * spread, 2 * spread), np.float32)
    pairing[
        col, col % experts_n * pair_w + col // spread * part_f + col % spread // experts_n
    ] = 1.0
    grad_gu = dot(grad_gu, jnp.asarray(pairing, BF), 1, 0).astype(BF)
    grad_gu = grad_gu.reshape(N_XH * N_C, own_d, experts_n, pair_w).transpose(0, 2, 1, 3)
    parts = jnp.concatenate(
        [
            grad_gu.reshape(N_XH, N_C, experts_n * own_d, pair_w),
            grad_dn.reshape(N_XH, N_C, -1, LANES),
        ],
        axis=2,
    )
    parts = to_owners(owner_sums(parts.reshape(N_XH, -1, LANES)))
    in_grad = scatter_chips(scatter_cores(in_part.astype(BF).reshape(N_GROUP, rows, model_w)))
    grad_dense = lax.psum_scatter(grad_dense, "z", scatter_dimension=0, tiled=True)
    dense_parts = spread_sums(after(grad_dense, parts))
    inv_in = lax.rsqrt(jnp.mean(x_own * x_own, axis=1, keepdims=True) + EPSILON)
    unit_in = x_own * inv_in
    scaled_in = in_grad * gain_in[None, :]
    tokens_grad = mixed_grad + inv_in * (
        scaled_in - unit_in * jnp.mean(scaled_in * unit_in, axis=1, keepdims=True)
    )

    gu_lines = experts_n * own_d
    g_ids = jnp.arange(N_GROUP * part_f, dtype=jnp.int32)[:, None]
    h_ids = g_ids % part_f
    place = own_f * (h_ids // part_down) + part_down * (g_ids // part_f) + h_ids % part_down
    spread_out = (place == jnp.arange(hidden_w, dtype=jnp.int32)[None, :]).astype(BF)
    pairs = parts[:, :gu_lines].reshape(N_GROUP, gu_lines, 2, part_f)

    def side_gu(k):
        x = pairs[:, :, k].transpose(1, 0, 2).reshape(gu_lines, N_GROUP * part_f)
        x = dot(x, spread_out, 1, 0)
        return x.reshape(experts_n, own_d, hidden_w).transpose(1, 0, 2)

    grad_w_gate, grad_w_up = side_gu(0), side_gu(1)
    grad_w_down = parts[:, gu_lines:].astype(F32)
    grad_w_down = grad_w_down.reshape(own_f, experts_n, model_w)

    def side(at, width):
        return dense_parts[:, :, at : at + width].transpose(1, 0, 2).reshape(own_d, -1)

    grad_w_query = side(0, q_w)
    grad_w_key = side(q_w, kv_w)
    grad_w_value = side(qk_w, kv_w)
    grad_w_out = side(qkv_w, out_w)
    aux_grad = jnp.sum(dense_parts[:, :, qkv_w + out_w :], axis=0)
    return (
        output,
        tokens_grad,
        aux_grad[:, experts_n],
        grad_w_query,
        grad_w_key,
        grad_w_value,
        grad_w_out,
        aux_grad[:, experts_n + 1],
        aux_grad[:, :experts_n],
        grad_w_gate,
        grad_w_up,
        grad_w_down,
    )


def solution(mesh):
    split = Mesh(mesh.devices.reshape([SIZES[k] for k in REP_SHARD]), REP_SHARD)
    placed = (
        P(REP_SHARD, None),
        P(REP_SHARD, None),
        P(REP_SHARD, None),
        P(REP_SHARD, None),
        P(SHARD),
        P(SHARD, None),
        P(SHARD, None),
        P(SHARD, None),
        P(SHARD, None),
        P(SHARD),
        P(SHARD, None),
        P(SHARD, None, None),
        P(SHARD, None, None),
        P(SHARD, None, None),
    )
    return jax.shard_map(
        on_device,
        mesh=split,
        in_specs=placed,
        out_specs=(
            P(REP_SHARD, None),
            P(REP_SHARD, None),
            P(SHARD),
            P(SHARD, None),
            P(SHARD, None),
            P(SHARD, None),
            P(SHARD, None),
            P(SHARD),
            P(SHARD, None),
            P(SHARD, None, None),
            P(SHARD, None, None),
            P(SHARD, None, None),
        ),
        check_vma=False,
    )
```
